1024 devices in a mesh: layer: 4 (over x_hi, core), tok: 256 (over y, z, x_lo).
Axes of the slice: x: 4 (x_hi: 2, x_lo: 2; x = x_hi * 2 + x_lo), y: 8, z: 16, core: 2. Of those that a mesh axis runs over, the one named last changes fastest.
Arguments:
- acts: bfloat16 [4, 65536, 2304], P('layer', 'tok'), may hold values from -6 to 6
- w_enc: bfloat16 [4, 2304, 16384], P('layer', None, 'tok'), may hold values from -0.0625 to 0.0625
- b_enc: float32 [16384], P('tok'), may hold values from -3 to 3
- w_dec: bfloat16 [4, 16384, 2304], P('layer', 'tok'), may hold values from -0.375 to 0.375
- b_dec: float32 [4, 2304], P('layer'), may hold values from -3 to 3
Outputs:
- latents: bfloat16 [65536, 512], P('tok')
- recon: bfloat16 [4, 65536, 2304], P('layer', 'tok')
The draws below stay inside these ranges and needn't reach their ends.
All inputs are finite; a program needn't handle non-finite values.
Results may differ from the reference program's by a relative error of at most 0.017.
Values may be sent and summed in bfloat16 or wider, within the bound.
A program may use at most 32 MiB of HBM per device.

```python
import jax
import jax.numpy as jnp
from jax import lax

D = 2304
GROUP = 64
WINDOW = 8
TOK_DEV = 256
LAYERS = 4
TOKENS = 65536
LATENTS = 16384


def block_levels(own_key, extent, cuts, least, high):
    factor_of = 1.0
    for axis_at, parts in cuts:
        steps = jax.random.uniform(jax.random.fold_in(jax.random.fold_in(own_key, 6), axis_at), (parts,), jnp.float32, least / len(cuts), high / len(cuts))
        factor_of = factor_of * jnp.repeat(jnp.exp(steps), extent[axis_at] // parts).reshape((-1,) + (1,) * (len(extent) - 1 - axis_at))
    return factor_of


def bell_draw(key, extent, spread, reach, shards=(), kind=jnp.bfloat16):
    result = jax.random.normal(key, extent, jnp.float32) * spread
    if len(shards) > 0:
        result = block_levels(key, extent, shards, -0.22, 0.18) * result
    return jnp.clip(result, min=-reach, max=reach).astype(kind)


def setup_inputs(seed: int = 0) -> dict:
    splits = jax.random.split(jax.random.key(seed), 6)
    acts = bell_draw(splits[0], (LAYERS, TOKENS, D), 1.0, 6.0, ((0, 4), (1, 256)))
    w_enc = bell_draw(splits[1], (LAYERS, D, LATENTS), (4 * D) ** -0.5, 0.0625, ((0, 4), (2, 256)))
    b_enc = bell_draw(splits[2], (LATENTS,), 0.5, 3.0, ((0, 256),), jnp.float32)
    w_dec = bell_draw(splits[3], (LAYERS, LATENTS, D), (WINDOW * GROUP // 2) ** -0.5, 0.375, ((0, 4), (1, 256)))
    b_dec = bell_draw(splits[4], (LAYERS, D), 0.5, 3.0, ((0, 4),), jnp.float32)
    return {"acts": acts, "w_enc": w_enc, "b_enc": b_enc, "w_dec": w_dec, "b_dec": b_dec}


def reference(acts, w_enc, b_enc, w_dec, b_dec):
    blocks = TOKENS // TOK_DEV
    inner = jnp.arange(WINDOW * GROUP, dtype=jnp.int32)

    def one_block(tblock):
        shifts = inner // GROUP
        cols = (((tblock - shifts) % blocks) * GROUP + inner % GROUP).astype(jnp.int32)
        rows = lax.dynamic_slice_in_dim(acts, (tblock * TOK_DEV).astype(jnp.int32), TOK_DEV, 1)
        enc_win = jnp.take(w_enc, cols, axis=2)
        pre = jnp.zeros((TOK_DEV, WINDOW * GROUP), jnp.float32)
        for level in range(LAYERS):
            pre = pre + jnp.dot(rows[level], enc_win[level], preferred_element_type=jnp.float32)
        pre = pre + jnp.take(b_enc, cols, axis=0)
        lat = jnp.maximum(pre, 0.0).astype(jnp.bfloat16)
        dec_win = jnp.take(w_dec, cols, axis=1)
        outs = []
        for level in range(LAYERS):
            part = jnp.dot(lat, dec_win[level], preferred_element_type=jnp.float32) + b_dec[level]
            outs.append(part.astype(jnp.bfloat16))
        return lat, jnp.stack(outs)

    lat_all, rec_all = lax.map(one_block, jnp.arange(blocks, dtype=jnp.int32))
    latents = lat_all.reshape(TOKENS, WINDOW * GROUP)
    recon = jnp.transpose(rec_all, (1, 0, 2, 3)).reshape(LAYERS, TOKENS, D)
    return latents, recon
```

```python
import functools

import jax
import jax.numpy as jnp
from jax import lax
from jax.experimental import pallas as pl
from jax.experimental.pallas import tpu as pltpu
from jax.sharding import PartitionSpec as P

GROUP = 64
WINDOW = 8
MESH = pl.DeviceIdType.MESH


def chunk_plan(half):
    widths = [384, 384, 256, 128] if half == 1152 else [half]
    plan, at = [], 0
    for width in widths:
        plan.append((at, width))
        at += width
    return plan


def sem_plan(chunks):
    sizes = dict(enc=9, decx=2, dec=4 * chunks, acts=2, bias=5, bdec=2, sib=1,
                 part=3, gather=3, lat=4, rec=2 * chunks, out=1)
    at, plan = 0, {}
    for name, size in sizes.items():
        plan[name] = at
        at += size
    return plan, at


def kernel(ring, acts, enc, bias, dec, bdec, lat_out, rec_out,
           acts_all, enc_all, dec_all, bias_all, bd_all, pre, total, sib_out, sib_in,
           part_out, part_in, lat, rec, send, recv):
    rows, width = acts.shape
    half = width // 2
    quarter = rows // 4
    window = WINDOW * GROUP
    plan = chunk_plan(half)
    base, _ = sem_plan(len(plan))

    layer = lax.axis_index("layer")
    tok = lax.axis_index("tok")
    g, h = layer // 2, layer % 2
    m2, s = tok - tok % 2, tok % 2
    chip = 2 * g + s
    oh, os = 1 - h, 1 - s
    alone = h == s

    def at_site(g_, h_, s_):
        return (2 * g_ + h_, m2 + s_)

    following = (layer, lax.rem(tok + 2, ring))
    before = (layer, lax.rem(tok + ring - 2, ring))
    sibling = at_site(g, oh, s)

    pending = []

    def remote(src, dst, target, sem):
        return pltpu.make_async_remote_copy(
            src_ref=src, dst_ref=dst, send_sem=send.at[len(pending)], recv_sem=recv.at[sem],
            device_id=target, device_id_type=MESH)

    def push(src, dst, target, sem):
        copy = remote(src, dst, target, sem)
        copy.start()
        pending.append((None, copy))

    def push_or_keep(src, dst, target, sem, keep):
        away = jnp.logical_not(keep)
        copy = remote(src, dst, target, sem)

        @pl.when(away)
        def _():
            copy.start()

        @pl.when(keep)
        def _():
            pltpu.make_async_copy(src, dst, recv.at[sem]).start()

        pending.append((away, copy))

    def arrived(dst, sem):
        pltpu.make_async_copy(dst, dst, recv.at[sem]).wait()

    def lanes(d):
        return pl.ds(pl.multiple_of(d * half, half), half)

    def block(b, count=1):
        if isinstance(b, int):
            return pl.ds(b * GROUP, count * GROUP)
        return pl.ds(pl.multiple_of(b * GROUP, GROUP), count * GROUP)

    own_bias = bias[...]
    bias_all[os] = jnp.broadcast_to(jnp.concatenate([own_bias, own_bias], axis=1), (8, 2 * GROUP))

    barrier = pltpu.get_barrier_semaphore()
    me = 2 * chip + h
    for j in range(1, 8):
        other = lax.rem(me + j, 8)
        pl.semaphore_signal(barrier, inc=1, device_id=at_site(other // 4, other % 2, (other // 2) % 2),
                            device_id_type=MESH)
    for other in (following, before):
        pl.semaphore_signal(barrier, inc=1, device_id=other, device_id_type=MESH)
    pl.semaphore_wait(barrier, 9)

    def exchange(src, dst, sem):
        push(src.at[:, lanes(oh)], dst, at_site(g, oh, h), sem)
        push_or_keep(src.at[:, lanes(h)], dst, at_site(g, h, h), sem, alone)

    exchange(enc, enc_all.at[block(os)], base["enc"] + os)
    push(bias_all.at[os], bias_all.at[os], at_site(g, h, os), base["bias"])

    def enc_wait(b):
        arrived(enc_all.at[block(b)], base["enc"] + b)

    def enc_send(b):
        push(enc_all.at[block(b)], enc_all.at[block(b + 2)], following, base["enc"] + b + 2)

    def bias_pass(i):
        if i == 0:
            arrived(bias_all.at[s], base["bias"])
        else:
            arrived(bias_all.at[pl.ds(2 * i, 2)], base["bias"] + i)
        count = 1 if i == 3 else 2
        push(bias_all.at[pl.ds(2 * i, count)], bias_all.at[pl.ds(2 * i + 2, count)], following,
             base["bias"] + i + 1)

    enc_wait(os)
    enc_send(os)
    enc_wait(s)
    enc_send(s)
    bias_pass(0)

    exchange(dec, dec_all.at[block(os)], base["decx"] + s)
    exchange(acts, acts_all.at[s], base["acts"] + s)
    push(bdec.at[:, lanes(oh)], bd_all.at[1], sibling, base["bdec"] + 1)
    pltpu.make_async_copy(bdec.at[:, lanes(h)], bd_all.at[0], recv.at[base["bdec"]]).start()

    for i in (1, 2):
        for b in (2 * i + os, 2 * i + s):
            enc_wait(b)
            enc_send(b)
        bias_pass(i)
    enc_wait(6)
    enc_send(6)
    bias_pass(3)

    def dec_part(b, count, c):
        off, wide = plan[c]
        return dec_all.at[pl.ds(b * GROUP, count * GROUP), pl.ds(off, wide)]

    def dec_sem(c, i):
        return base["dec"] + 4 * c + i - 1

    def dec_send(i, c):
        if i > 0:
            arrived(dec_part(2 * i, 2, c), dec_sem(c, i))
        count = 1 if i == 3 else 2
        push(dec_part(2 * i, count, c), dec_part(2 * i + 2, count, c), following, dec_sem(c, i + 1))

    for p in (0, 1):
        arrived(dec_all.at[block(1 - p)], base["decx"] + p)
    for c in range(len(plan)):
        dec_send(0, c)

    arrived(acts_all.at[0], base["acts"])
    arrived(acts_all.at[1], base["acts"] + 1)

    def encode(t, q):
        first = (1 - t) * GROUP + q * (window // 2)
        pre[t, :, q * (window // 2):(q + 1) * (window // 2)] = lax.dot_general(
            acts_all[t], enc_all[first:first + window // 2, :], (((1,), (1,)), ((), ())),
            preferred_element_type=jnp.float32)

    steps = [(i, c) for c in range(len(plan)) for i in (1, 2, 3)]
    steps.sort(key=lambda step: (step[0] + step[1], step[1]))
    done = []

    def pass_on(count):
        for _ in range(count):
            if steps:
                step = steps.pop(0)
                dec_send(*step)
                done.append(step)

    encode(1, 0)
    encode(0, 0)
    enc_wait(7)
    encode(1, 1)
    enc_wait(8)
    encode(0, 1)

    sib_out[...] = pre[oh].astype(jnp.bfloat16)
    push(sib_out, sib_in, sibling, base["sib"])
    pass_on(2)
    arrived(sib_in, base["sib"])
    total[...] = pre[h] + sib_in[...].astype(jnp.float32)
    part_out[...] = total[...].astype(jnp.bfloat16)

    def chip_rows(c_):
        return pl.ds(pl.multiple_of(c_ * quarter, quarter), quarter)

    for j in (1, 3, 2):
        other = lax.rem(chip + j, 4)
        push(part_out.at[chip_rows(other)], part_in.at[j - 1], at_site(other // 2, h, other % 2),
             base["part"] + j - 1)
    pass_on(2)
    arrived(bias_all.at[pl.ds(8, 1)], base["bias"] + 4)
    low = lax.broadcasted_iota(jnp.int32, (1, 2 * GROUP), 1) < GROUP
    first = 1 - h
    bias_row = jnp.concatenate(
        [jnp.where(low, bias_all[first + k, 0:1, :], bias_all[first + k + 1, 0:1, :])
         for k in range(0, WINDOW, 2)], axis=1)
    for j in (1, 2, 3):
        arrived(part_in.at[j - 1], base["part"] + j - 1)
    value = total[chip_rows(chip), :] + bias_row
    for j in (1, 2, 3):
        value = value + part_in[j - 1].astype(jnp.float32)
    lat[h, chip_rows(chip), :] = jnp.maximum(value, 0.0).astype(jnp.bfloat16)

    mine = lat.at[h, chip_rows(chip)]
    for j in (1, 3, 2):
        other = lax.rem(chip + j, 4)
        push(mine, mine, at_site(other // 2, h, other % 2), base["gather"] + j - 1)
    push(mine, mine, sibling, base["lat"])
    pass_on(3)
    for j in (1, 3, 2):
        piece = lat.at[h, chip_rows(lax.rem(chip + 4 - j, 4))]
        arrived(piece, base["gather"] + j - 1)
        push(piece, piece, sibling, base["lat"] + j)
    pass_on(1)
    for j in (0, 1, 3, 2):
        arrived(lat.at[oh, chip_rows(lax.rem(chip + 4 - j, 4))], base["lat"] + j)
    latents_copy = pltpu.make_async_copy(lat.at[s], lat_out, recv.at[base["out"]])
    latents_copy.start()

    arrived(bd_all.at[0], base["bdec"])
    arrived(bd_all.at[1], base["bdec"] + 1)
    shift = jnp.where(alone, bd_all[0], bd_all[1])

    def decode(c):
        off, wide = plan[c]
        while (3, c) not in done:
            pass_on(1)
        arrived(dec_part(8, 1, c), dec_sem(c, 4))
        for t in (0, 1):
            first = (1 - t) * GROUP
            value = jnp.dot(lat[t], dec_all[first:first + window, off:off + wide],
                            preferred_element_type=jnp.float32)
            value = value + shift[:, off:off + wide]
            rec[t, :, off:off + wide] = value.astype(jnp.bfloat16)
            keep = jnp.logical_and(alone, s == t)
            to = rec_out.at[:, pl.ds(pl.multiple_of(h * half + off, 128), wide)]
            push_or_keep(rec.at[t, :, pl.ds(off, wide)], to, at_site(g, s, t),
                         base["rec"] + 2 * c + h, keep)

    for c in range(len(plan)):
        decode(c)

    for c, (off, wide) in enumerate(plan):
        for d in (0, 1):
            arrived(rec_out.at[:, pl.ds(d * half + off, wide)], base["rec"] + 2 * c + d)
    latents_copy.wait()
    for away, copy in pending:
        if away is None:
            copy.wait_send()
        else:
            pl.when(away)(copy.wait_send)


def on_device(acts, w_enc, b_enc, w_dec, b_dec):
    ring = lax.axis_size("tok")
    rows, width = acts.shape[1:]
    half = width // 2
    window = WINDOW * GROUP
    chunks = len(chunk_plan(half))
    blocks = WINDOW + 1
    hbm = pl.BlockSpec(memory_space=pl.ANY)
    vmem = pl.BlockSpec(memory_space=pltpu.VMEM)
    bf16, f32 = jnp.bfloat16, jnp.float32
    latents, recon = pl.pallas_call(
        functools.partial(kernel, ring),
        out_shape=(
            jax.ShapeDtypeStruct((rows, window), bf16),
            jax.ShapeDtypeStruct((rows, width), bf16),
        ),
        in_specs=[hbm, hbm, vmem, hbm, hbm],
        out_specs=(hbm, hbm),
        scratch_shapes=[
            pltpu.VMEM((2, rows, half), bf16),
            pltpu.VMEM((blocks * GROUP, half), bf16),
            pltpu.VMEM((blocks * GROUP, half), bf16),
            pltpu.VMEM((blocks, 8, 2 * GROUP), f32),
            pltpu.VMEM((2, 1, half), f32),
            pltpu.VMEM((2, rows, window), f32),
            pltpu.VMEM((rows, window), f32),
            pltpu.VMEM((rows, window), bf16),
            pltpu.VMEM((rows, window), bf16),
            pltpu.VMEM((rows, window), bf16),
            pltpu.VMEM((3, rows // 4, window), bf16),
            pltpu.VMEM((2, rows, window), bf16),
            pltpu.VMEM((2, rows, half), bf16),
            pltpu.SemaphoreType.DMA((40 + 6 * chunks,)),
            pltpu.SemaphoreType.DMA((sem_plan(chunks)[1],)),
        ],
        compiler_params=pltpu.CompilerParams(
            collective_id=0, has_side_effects=True, vmem_limit_bytes=40 * 1024 * 1024
        ),
        cost_estimate=pl.CostEstimate(
            flops=4 * rows * window * width, bytes_accessed=8 * rows * width, transcendentals=0
        ),
    )(acts[0], jnp.swapaxes(w_enc[0], 0, 1), b_enc.reshape(1, GROUP), w_dec[0], b_dec)
    return latents, recon[None]


def solution(mesh):
    return jax.shard_map(
        on_device,
        mesh=mesh,
        in_specs=(
            P("layer", "tok", None),
            P("layer", None, "tok"),
            P("tok"),
            P("layer", "tok", None),
            P("layer", None),
        ),
        out_specs=(P("tok", None), P("layer", "tok", None)),
        check_vma=False,
    )
```

```python
import functools

import jax
import jax.numpy as jnp
from jax import lax
from jax.experimental import pallas as pl
from jax.experimental.pallas import tpu as pltpu
from jax.sharding import PartitionSpec as P

GROUP = 64
WINDOW = 8
MESH = pl.DeviceIdType.MESH
ENC_WIDTHS = [640, 512]
DEC_WIDTHS = [384, 384, 384]


def column_plan(half, widths):
    if half != sum(widths):
        widths = [half]
    plan, at = [], 0
    for width in widths:
        plan.append((at, width))
        at += width
    return plan


def sem_plan(enc_pieces, dec_pieces):
    sizes = dict(own=2, enc=9 * enc_pieces, acts=2, bias=5, sib=2, part=6, gather=6, lat=8,
                 kept=1, half=2, dec=4 * dec_pieces, decx=4 * dec_pieces, out=1)
    at, plan = 0, {}
    for name, size in sizes.items():
        plan[name] = at
        at += size
    return plan, at


def kernel(ring, acts, enc, bias, dec, lat_out, dec_win,
           acts_all, enc_all, bias_all, pre, total, sib_out, sib_in,
           part_out, part_in, lat, send, recv):
    rows, width = acts.shape
    half = width // 2
    quarter = rows // 4
    window = WINDOW * GROUP
    part = window // 2
    enc_plan, dec_plan = column_plan(half, ENC_WIDTHS), column_plan(half, DEC_WIDTHS)
    base, _ = sem_plan(len(enc_plan), len(dec_plan))

    layer = lax.axis_index("layer")
    tok = lax.axis_index("tok")
    g, h = layer // 2, layer % 2
    m2, s = tok - tok % 2, tok % 2
    chip = 2 * g + s
    oh, os = 1 - h, 1 - s
    alone = h == s

    def at_site(g_, h_, s_):
        return (2 * g_ + h_, m2 + s_)

    following = (layer, lax.rem(tok + 2, ring))
    before = (layer, lax.rem(tok + ring - 2, ring))
    sibling = at_site(g, oh, s)
    across = at_site(g, h, os)

    pending = []

    def remote(src, dst, target, sem):
        return pltpu.make_async_remote_copy(
            src_ref=src, dst_ref=dst, send_sem=send.at[len(pending)], recv_sem=recv.at[sem],
            device_id=target, device_id_type=MESH)

    def push(src, dst, target, sem):
        copy = remote(src, dst, target, sem)
        copy.start()
        pending.append((None, copy))

    def push_if(cond, src, dst, target, sem):
        copy = remote(src, dst, target, sem)
        pl.when(cond)(copy.start)
        pending.append((cond, copy))

    def push_or_keep(src, dst, target, sem, keep):
        away = jnp.logical_not(keep)
        copy = remote(src, dst, target, sem)

        @pl.when(away)
        def _():
            copy.start()

        @pl.when(keep)
        def _():
            pltpu.make_async_copy(src, dst, recv.at[sem]).start()

        pending.append((away, copy))

    def arrived(dst, sem):
        pltpu.make_async_copy(dst, dst, recv.at[sem]).wait()

    def lanes(d):
        return pl.ds(pl.multiple_of(d * half, half), half)

    def block(b, count=1):
        if isinstance(b, int):
            return pl.ds(b * GROUP, count * GROUP)
        return pl.ds(pl.multiple_of(b * GROUP, GROUP), count * GROUP)

    own_bias = bias[...]
    bias_all[os] = jnp.broadcast_to(jnp.concatenate([own_bias, own_bias], axis=1), (8, 2 * GROUP))

    barrier = pltpu.get_barrier_semaphore()
    me = 2 * chip + h
    for j in range(1, 8):
        other = lax.rem(me + j, 8)
        pl.semaphore_signal(barrier, inc=1, device_id=at_site(other // 4, other % 2, (other // 2) % 2),
                            device_id_type=MESH)
    pl.semaphore_signal(barrier, inc=1, device_id=before, device_id_type=MESH)
    pl.semaphore_wait(barrier, 8)

    def exchange(src, dst, sem):
        push(src.at[:, lanes(oh)], dst, at_site(g, oh, h), sem)
        push_or_keep(src.at[:, lanes(h)], dst, at_site(g, h, h), sem, alone)

    pltpu.make_async_copy(dec, dec_win.at[block(os)], recv.at[base["kept"]]).start()
    exchange(enc, enc_all.at[block(os)], base["own"] + s)
    push(bias_all.at[os], bias_all.at[os], across, base["bias"])

    def enc_part(b, e):
        off, wide = enc_plan[e]
        return enc_all.at[block(b), pl.ds(off, wide)]

    def enc_wait(b, e):
        arrived(enc_part(b, e), base["enc"] + len(enc_plan) * b + e)

    def enc_send(b, e):
        push(enc_part(b, e), enc_part(b + 2, e), following, base["enc"] + len(enc_plan) * (b + 2) + e)

    def enc_pass(b):
        for e in range(len(enc_plan)):
            enc_wait(b, e)
            enc_send(b, e)

    def enc_own(b, p):
        arrived(enc_all.at[block(b)], base["own"] + p)
        for e in range(len(enc_plan)):
            enc_send(b, e)

    def bias_pass(i):
        if i == 0:
            arrived(bias_all.at[s], base["bias"])
        else:
            arrived(bias_all.at[pl.ds(2 * i, 2)], base["bias"] + i)
        count = 1 if i == 3 else 2
        push(bias_all.at[pl.ds(2 * i, count)], bias_all.at[pl.ds(2 * i + 2, count)], following,
             base["bias"] + i + 1)

    enc_own(os, s)
    enc_own(s, os)
    push(dec.at[:, lanes(os)], dec_win.at[block(os), lanes(os)], across, base["half"])
    exchange(acts, acts_all.at[s], base["acts"] + s)
    push_if(s == 0, dec.at[:, lanes(0)], dec_win.at[block(1), lanes(0)], across, base["half"] + 1)
    bias_pass(0)

    for i in (1, 2):
        enc_pass(2 * i + os)
        enc_pass(2 * i + s)
        bias_pass(i)
    enc_pass(6)
    bias_pass(3)

    def columns(q):
        return pl.ds(q * part, part)

    def encode(t, q):
        first = (1 - t) * GROUP + q * part
        pre[t, :, q * part:(q + 1) * part] = lax.dot_general(
            acts_all[t], enc_all[first:first + part, :], (((1,), (1,)), ((), ())),
            preferred_element_type=jnp.float32)

    def cores_send(q):
        sib_out[q] = pre[oh, :, q * part:(q + 1) * part].astype(jnp.bfloat16)
        push(sib_out.at[q], sib_in.at[q], sibling, base["sib"] + q)

    def chip_rows(c_):
        return pl.ds(pl.multiple_of(c_ * quarter, quarter), quarter)

    def chips_send(q):
        arrived(sib_in.at[q], base["sib"] + q)
        value = pre[h, :, q * part:(q + 1) * part] + sib_in[q].astype(jnp.float32)
        total[:, q * part:(q + 1) * part] = value
        part_out[:, q * part:(q + 1) * part] = value.astype(jnp.bfloat16)
        for j in (2, 1, 3):
            other = lax.rem(chip + j, 4)
            push(part_out.at[chip_rows(other), columns(q)], part_in.at[3 * q + j - 1],
                 at_site(other // 2, h, other % 2), base["part"] + 3 * q + j - 1)

    def latents_send(q):
        value = total[chip_rows(chip), q * part:(q + 1) * part] + bias_row[:, q * part:(q + 1) * part]
        for j in (1, 3, 2):
            arrived(part_in.at[3 * q + j - 1], base["part"] + 3 * q + j - 1)
            value = value + part_in[3 * q + j - 1].astype(jnp.float32)
        lat[h, chip_rows(chip), q * part:(q + 1) * part] = jnp.maximum(value, 0.0).astype(jnp.bfloat16)
        mine = lat.at[h, chip_rows(chip), columns(q)]
        for j in (2, 1, 3):
            other = lax.rem(chip + j, 4)
            push(mine, mine, at_site(other // 2, h, other % 2), base["gather"] + 3 * q + j - 1)
        push(mine, mine, sibling, base["lat"] + 4 * q)

    def latents_share(q):
        for j in (1, 3, 2):
            piece = lat.at[h, chip_rows(lax.rem(chip + 4 - j, 4)), columns(q)]
            arrived(piece, base["gather"] + 3 * q + j - 1)
            push(piece, piece, sibling, base["lat"] + 4 * q + j)

    def latents_wait(q):
        for j in (0, 1, 3, 2):
            arrived(lat.at[oh, chip_rows(lax.rem(chip + 4 - j, 4)), columns(q)], base["lat"] + 4 * q + j)

    def dec_part(b, count, c, side):
        off, wide = dec_plan[c]
        return dec_win.at[pl.ds(b * GROUP, count * GROUP),
                          pl.ds(pl.multiple_of(side * half + off, 128), wide)]

    def dec_sem(kind, i, c):
        return base[kind] + len(dec_plan) * (i - 1) + c

    def dec_pass(i):
        count = 1 if i == 3 else 2
        for c in range(len(dec_plan)):
            if i > 0:
                arrived(dec_part(2 * i, 2, c, s), dec_sem("dec", i, c))
            push(dec_part(2 * i, count, c, s), dec_part(2 * i + 2, count, c, s), following,
                 dec_sem("dec", i + 1, c))
            if i > 0:
                push(dec_part(2 * i, 2, c, s), dec_part(2 * i, 2, c, s), across, dec_sem("decx", i, c))

    arrived(dec_win.at[block(os)], base["kept"])
    arrived(dec_win.at[block(s), lanes(s)], base["half"])
    dec_pass(0)

    arrived(acts_all.at[0], base["acts"])
    arrived(acts_all.at[1], base["acts"] + 1)
    encode(1, 0)
    encode(0, 0)
    cores_send(0)
    for e in range(len(enc_plan)):
        enc_wait(7, e)
    encode(1, 1)
    arrived(bias_all.at[pl.ds(8, 1)], base["bias"] + 4)
    low = lax.broadcasted_iota(jnp.int32, (1, 2 * GROUP), 1) < GROUP
    bias_row = jnp.concatenate(
        [jnp.where(low, bias_all[oh + k, 0:1, :], bias_all[oh + k + 1, 0:1, :])
         for k in range(0, WINDOW, 2)], axis=1)
    chips_send(0)
    for e in range(len(enc_plan)):
        enc_wait(8, e)
    encode(0, 1)
    cores_send(1)
    dec_pass(1)
    chips_send(1)
    latents_send(0)
    dec_pass(2)
    latents_send(1)
    latents_share(0)
    dec_pass(3)
    latents_share(1)
    latents_wait(0)
    latents_wait(1)
    latents_copy = pltpu.make_async_copy(lat.at[s], lat_out, recv.at[base["out"]])
    latents_copy.start()
    for c in range(len(dec_plan)):
        arrived(dec_part(8, 1, c, s), dec_sem("dec", 4, c))
        push_if(s == 1, dec_part(8, 1, c, 1), dec_part(8, 1, c, 1), across, dec_sem("decx", 4, c))

    @pl.when(s == 1)
    def _():
        arrived(dec_win.at[block(1), lanes(0)], base["half"] + 1)

    for i in (1, 2, 3):
        for c in range(len(dec_plan)):
            arrived(dec_part(2 * i, 2, c, os), dec_sem("decx", i, c))

    @pl.when(s == 0)
    def _():
        for c in range(len(dec_plan)):
            arrived(dec_part(8, 1, c, 1), dec_sem("decx", 4, c))

    latents_copy.wait()
    for away, copy in pending:
        if away is None:
            copy.wait_send()
        else:
            pl.when(away)(copy.wait_send)


def decode(lat, dec_win, bdec, lat_out, rec_out):
    first = pl.multiple_of((1 - lax.axis_index("tok") % 2) * GROUP, GROUP)
    value = jnp.dot(lat[...], dec_win[pl.ds(first, lat.shape[1]), :], preferred_element_type=jnp.float32)
    rec_out[...] = (value + bdec[...]).astype(jnp.bfloat16)

    @pl.when(pl.program_id(0) == 0)
    def _():
        lat_out[...] = lat[...]


def on_device(acts, w_enc, b_enc, w_dec, b_dec):
    ring = lax.axis_size("tok")
    rows, width = acts.shape[1:]
    half = width // 2
    window = WINDOW * GROUP
    blocks = WINDOW + 1
    _, arrivals = sem_plan(len(column_plan(half, ENC_WIDTHS)), len(column_plan(half, DEC_WIDTHS)))
    hbm = pl.BlockSpec(memory_space=pl.ANY)
    vmem = pl.BlockSpec(memory_space=pltpu.VMEM)
    bf16, f32 = jnp.bfloat16, jnp.float32
    latents, dec_win = pl.pallas_call(
        functools.partial(kernel, ring),
        out_shape=(
            jax.ShapeDtypeStruct((rows, window), bf16),
            jax.ShapeDtypeStruct((blocks * GROUP, width), bf16),
        ),
        in_specs=[hbm, hbm, vmem, hbm],
        out_specs=(hbm, hbm),
        scratch_shapes=[
            pltpu.VMEM((2, rows, half), bf16),
            pltpu.VMEM((blocks * GROUP, half), bf16),
            pltpu.VMEM((blocks, 8, 2 * GROUP), f32),
            pltpu.VMEM((2, rows, window), f32),
            pltpu.VMEM((rows, window), f32),
            pltpu.VMEM((2, rows, window // 2), bf16),
            pltpu.VMEM((2, rows, window // 2), bf16),
            pltpu.VMEM((rows, window), bf16),
            pltpu.VMEM((6, rows // 4, window // 2), bf16),
            pltpu.VMEM((2, rows, window), bf16),
            pltpu.SemaphoreType.DMA((80,)),
            pltpu.SemaphoreType.DMA((arrivals,)),
        ],
        compiler_params=pltpu.CompilerParams(
            collective_id=0, has_side_effects=True, vmem_limit_bytes=60 * 1024 * 1024
        ),
        cost_estimate=pl.CostEstimate(
            flops=2 * rows * window * width, bytes_accessed=8 * rows * width, transcendentals=0
        ),
    )(acts[0], jnp.swapaxes(w_enc[0], 0, 1), b_enc.reshape(1, GROUP), w_dec[0])
    steps = 3 if width % 384 == 0 else 1
    wide = width // steps
    latents, recon = pl.pallas_call(
        decode,
        grid=(steps,),
        out_shape=(
            jax.ShapeDtypeStruct((rows, window), bf16),
            jax.ShapeDtypeStruct((rows, width), bf16),
        ),
        in_specs=[
            pl.BlockSpec((rows, window), lambda i: (0, 0)),
            pl.BlockSpec((blocks * GROUP, wide), lambda i: (0, i)),
            pl.BlockSpec((1, wide), lambda i: (0, i)),
        ],
        out_specs=(
            pl.BlockSpec((rows, window), lambda i: (0, 0)),
            pl.BlockSpec((rows, wide), lambda i: (0, i)),
        ),
        cost_estimate=pl.CostEstimate(
            flops=2 * rows * window * width, bytes_accessed=6 * rows * width, transcendentals=0
        ),
    )(latents, dec_win, b_dec)
    return latents, recon[None]


def solution(mesh):
    return jax.shard_map(
        on_device,
        mesh=mesh,
        in_specs=(
            P("layer", "tok", None),
            P("layer", None, "tok"),
            P("tok"),
            P("layer", "tok", None),
            P("layer", None),
        ),
        out_specs=(P("tok", None), P("layer", "tok", None)),
        check_vma=False,
    )
```

```python
import functools

import jax
import jax.numpy as jnp
from jax import lax
from jax.experimental import pallas as pl
from jax.experimental.pallas import tpu as pltpu
from jax.sharding import PartitionSpec as P

GROUP = 64
WINDOW = 8
MESH = pl.DeviceIdType.MESH
ENC_WIDTHS = [640, 512]
DEC_WIDTHS = [384, 384, 384]


def column_plan(half, widths):
    if half != sum(widths):
        widths = [half]
    plan, at = [], 0
    for width in widths:
        plan.append((at, width))
        at += width
    return plan


def sem_plan(enc_pieces, dec_pieces):
    sizes = dict(own=2, enc=9 * enc_pieces, acts=2, bias=5, sib=2, part=6, gather=6, lat=8,
                 kept=1, half=2, dec=4 * dec_pieces, decx=4 * dec_pieces, out=1)
    at, plan = 0, {}
    for name, size in sizes.items():
        plan[name] = at
        at += size
    return plan, at


def kernel(ring, acts, enc, bias, dec, lat_out, dec_win,
           acts_all, enc_all, bias_all, pre, total, sib_out, sib_in,
           part_out, part_in, lat, send, recv):
    rows, width = acts.shape
    half = width // 2
    quarter = rows // 4
    window = WINDOW * GROUP
    part = window // 2
    enc_plan, dec_plan = column_plan(half, ENC_WIDTHS), column_plan(half, DEC_WIDTHS)
    base, _ = sem_plan(len(enc_plan), len(dec_plan))

    layer = lax.axis_index("layer")
    tok = lax.axis_index("tok")
    g, h = layer // 2, layer % 2
    m2, s = tok - tok % 2, tok % 2
    chip = 2 * g + s
    oh, os = 1 - h, 1 - s
    alone = h == s

    def at_site(g_, h_, s_):
        return (2 * g_ + h_, m2 + s_)

    following = (layer, lax.rem(tok + 2, ring))
    before = (layer, lax.rem(tok + ring - 2, ring))
    sibling = at_site(g, oh, s)
    across = at_site(g, h, os)

    pending = []

    def remote(src, dst, target, sem):
        return pltpu.make_async_remote_copy(
            src_ref=src, dst_ref=dst, send_sem=send.at[len(pending)], recv_sem=recv.at[sem],
            device_id=target, device_id_type=MESH)

    settled = [0]

    def settle(count):
        for away, copy in pending[settled[0]:count]:
            if away is None:
                copy.wait_send()
            else:
                pl.when(away)(copy.wait_send)
        settled[0] = max(settled[0], count)

    def push(src, dst, target, sem):
        copy = remote(src, dst, target, sem)
        copy.start()
        pending.append((None, copy))

    def push_if(cond, src, dst, target, sem):
        copy = remote(src, dst, target, sem)
        pl.when(cond)(copy.start)
        pending.append((cond, copy))

    def push_or_keep(src, dst, target, sem, keep):
        away = jnp.logical_not(keep)
        copy = remote(src, dst, target, sem)

        @pl.when(away)
        def _():
            copy.start()

        @pl.when(keep)
        def _():
            pltpu.make_async_copy(src, dst, recv.at[sem]).start()

        pending.append((away, copy))

    def arrived(dst, sem):
        pltpu.make_async_copy(dst, dst, recv.at[sem]).wait()

    def lanes(d):
        return pl.ds(pl.multiple_of(d * half, half), half)

    def block(b, count=1):
        if isinstance(b, int):
            return pl.ds(b * GROUP, count * GROUP)
        return pl.ds(pl.multiple_of(b * GROUP, GROUP), count * GROUP)

    own_bias = bias[...]
    bias_all[os] = jnp.broadcast_to(jnp.concatenate([own_bias, own_bias], axis=1), (8, 2 * GROUP))

    barrier = pltpu.get_barrier_semaphore()
    me = 2 * chip + h
    for j in range(1, 8):
        other = lax.rem(me + j, 8)
        pl.semaphore_signal(barrier, inc=1, device_id=at_site(other // 4, other % 2, (other // 2) % 2),
                            device_id_type=MESH)
    pl.semaphore_signal(barrier, inc=1, device_id=before, device_id_type=MESH)
    pl.semaphore_wait(barrier, 8)

    def exchange(src, dst, sem):
        push(src.at[:, lanes(oh)], dst, at_site(g, oh, h), sem)
        push_or_keep(src.at[:, lanes(h)], dst, at_site(g, h, h), sem, alone)

    pltpu.make_async_copy(dec, dec_win.at[block(os)], recv.at[base["kept"]]).start()
    exchange(enc, enc_all.at[block(os)], base["own"] + s)
    push(bias_all.at[os], bias_all.at[os], across, base["bias"])

    def enc_part(b, e):
        off, wide = enc_plan[e]
        return enc_all.at[block(b), pl.ds(off, wide)]

    def enc_wait(b, e):
        arrived(enc_part(b, e), base["enc"] + len(enc_plan) * b + e)

    def enc_send(b, e):
        push(enc_part(b, e), enc_part(b + 2, e), following, base["enc"] + len(enc_plan) * (b + 2) + e)

    def enc_pass(b):
        for e in range(len(enc_plan)):
            enc_wait(b, e)
            enc_send(b, e)

    def enc_own(b, p, near):
        sem = base["enc"] + len(enc_plan) * (b + 2)
        if near:
            for e, (off, wide) in enumerate(enc_plan):
                here = enc.at[:, pl.ds(pl.multiple_of(h * half + off, 128), wide)]
                push_if(alone, here, enc_part(b + 2, e), following, sem + e)
        arrived(enc_all.at[block(b)], base["own"] + p)
        for e in range(len(enc_plan)):
            if near:
                push_if(jnp.logical_not(alone), enc_part(b, e), enc_part(b + 2, e), following, sem + e)
            else:
                enc_send(b, e)

    def bias_pass(i):
        if i == 0:
            arrived(bias_all.at[s], base["bias"])
        else:
            arrived(bias_all.at[pl.ds(2 * i, 2)], base["bias"] + i)
        count = 1 if i == 3 else 2
        push(bias_all.at[pl.ds(2 * i, count)], bias_all.at[pl.ds(2 * i + 2, count)], following,
             base["bias"] + i + 1)

    enc_own(os, s, True)
    enc_own(s, os, False)
    push(dec.at[:, lanes(os)], dec_win.at[block(os), lanes(os)], across, base["half"])
    exchange(acts, acts_all.at[s], base["acts"] + s)
    push_if(s == 0, dec.at[:, lanes(0)], dec_win.at[block(1), lanes(0)], across, base["half"] + 1)
    bias_pass(0)

    for i in (1, 2):
        enc_pass(2 * i + os)
        enc_pass(2 * i + s)
        bias_pass(i)
    enc_pass(6)
    bias_pass(3)

    def columns(q):
        return pl.ds(q * part, part)

    def encode(t, q):
        first = (1 - t) * GROUP + q * part
        pre[t, :, q * part:(q + 1) * part] = lax.dot_general(
            acts_all[t], enc_all[first:first + part, :], (((1,), (1,)), ((), ())),
            preferred_element_type=jnp.float32)

    def cores_send(q):
        sib_out[q] = pre[oh, :, q * part:(q + 1) * part].astype(jnp.bfloat16)
        push(sib_out.at[q], sib_in.at[q], sibling, base["sib"] + q)

    def chip_rows(c_):
        return pl.ds(pl.multiple_of(c_ * quarter, quarter), quarter)

    def chips_send(q):
        arrived(sib_in.at[q], base["sib"] + q)
        value = pre[h, :, q * part:(q + 1) * part] + sib_in[q].astype(jnp.float32)
        total[:, q * part:(q + 1) * part] = value
        part_out[:, q * part:(q + 1) * part] = value.astype(jnp.bfloat16)
        for j in (2, 1, 3):
            other = lax.rem(chip + j, 4)
            push(part_out.at[chip_rows(other), columns(q)], part_in.at[3 * q + j - 1],
                 at_site(other // 2, h, other % 2), base["part"] + 3 * q + j - 1)

    def latents_send(q):
        value = total[chip_rows(chip), q * part:(q + 1) * part] + bias_row[:, q * part:(q + 1) * part]
        for j in (1, 3, 2):
            arrived(part_in.at[3 * q + j - 1], base["part"] + 3 * q + j - 1)
            value = value + part_in[3 * q + j - 1].astype(jnp.float32)
        lat[h, chip_rows(chip), q * part:(q + 1) * part] = jnp.maximum(value, 0.0).astype(jnp.bfloat16)
        mine = lat.at[h, chip_rows(chip), columns(q)]
        for j in (2, 1, 3):
            other = lax.rem(chip + j, 4)
            push(mine, mine, at_site(other // 2, h, other % 2), base["gather"] + 3 * q + j - 1)
        push(mine, mine, sibling, base["lat"] + 4 * q)

    def latents_share(q):
        for j in (1, 3, 2):
            piece = lat.at[h, chip_rows(lax.rem(chip + 4 - j, 4)), columns(q)]
            arrived(piece, base["gather"] + 3 * q + j - 1)
            push(piece, piece, sibling, base["lat"] + 4 * q + j)

    def latents_wait(q):
        for j in (0, 1, 3, 2):
            arrived(lat.at[oh, chip_rows(lax.rem(chip + 4 - j, 4)), columns(q)], base["lat"] + 4 * q + j)

    def dec_part(b, count, c, side):
        off, wide = dec_plan[c]
        return dec_win.at[pl.ds(b * GROUP, count * GROUP),
                          pl.ds(pl.multiple_of(side * half + off, 128), wide)]

    def dec_sem(kind, i, c):
        return base[kind] + len(dec_plan) * (i - 1) + c

    def dec_pass(i, pieces=range(len(dec_plan))):
        count = 1 if i == 3 else 2
        for c in pieces:
            if i > 0:
                arrived(dec_part(2 * i, 2, c, s), dec_sem("dec", i, c))
            push(dec_part(2 * i, count, c, s), dec_part(2 * i + 2, count, c, s), following,
                 dec_sem("dec", i + 1, c))
            if i > 0:
                push(dec_part(2 * i, 2, c, s), dec_part(2 * i, 2, c, s), across, dec_sem("decx", i, c))

    arrived(dec_win.at[block(os)], base["kept"])
    arrived(dec_win.at[block(s), lanes(s)], base["half"])
    dec_pass(0)

    arrived(acts_all.at[0], base["acts"])
    arrived(acts_all.at[1], base["acts"] + 1)
    encode(1, 0)
    encode(0, 0)
    cores_send(0)
    for e in range(len(enc_plan)):
        enc_wait(7, e)
    encode(1, 1)
    arrived(bias_all.at[pl.ds(8, 1)], base["bias"] + 4)
    low = lax.broadcasted_iota(jnp.int32, (1, 2 * GROUP), 1) < GROUP
    bias_row = jnp.concatenate(
        [jnp.where(low, bias_all[oh + k, 0:1, :], bias_all[oh + k + 1, 0:1, :])
         for k in range(0, WINDOW, 2)], axis=1)
    chips_send(0)
    for e in range(len(enc_plan)):
        enc_wait(8, e)
    encode(0, 1)
    cores_send(1)
    sent = len(pending)
    dec_pass(1, [0])
    chips_send(1)
    dec_pass(1, [1])
    latents_send(0)
    dec_pass(1, range(2, len(dec_plan)))
    latents_send(1)
    latents_share(0)
    dec_pass(2, [0])
    dec_pass(2, [1])
    latents_share(1)
    dec_pass(2, range(2, len(dec_plan)))
    settle(sent)
    sent = len(pending)
    dec_pass(3)
    latents_wait(0)
    latents_wait(1)
    latents_copy = pltpu.make_async_copy(lat.at[s], lat_out, recv.at[base["out"]])
    latents_copy.start()
    for c in range(len(dec_plan)):
        arrived(dec_part(8, 1, c, s), dec_sem("dec", 4, c))
        push_if(s == 1, dec_part(8, 1, c, 1), dec_part(8, 1, c, 1), across, dec_sem("decx", 4, c))
    settle(sent)

    @pl.when(s == 1)
    def _():
        arrived(dec_win.at[block(1), lanes(0)], base["half"] + 1)

    for i in (1, 2, 3):
        for c in range(len(dec_plan)):
            arrived(dec_part(2 * i, 2, c, os), dec_sem("decx", i, c))

    @pl.when(s == 0)
    def _():
        for c in range(len(dec_plan)):
            arrived(dec_part(8, 1, c, 1), dec_sem("decx", 4, c))

    latents_copy.wait()
    settle(len(pending))


def decode(lat, dec_win, bdec, lat_out, rec_out, lat_here, win_here, bias_here, rec_here, came, left):
    window = lat.shape[1]
    first = pl.multiple_of((1 - lax.axis_index("tok") % 2) * GROUP, GROUP)
    steps = came.shape[0] - 2
    wide = dec_win.shape[1] // steps

    def columns(c):
        return pl.ds(c * wide, wide)

    coming = [pltpu.make_async_copy(lat, lat_here, came.at[0]), pltpu.make_async_copy(bdec, bias_here, came.at[1])]
    for c in range(steps):
        coming.append(pltpu.make_async_copy(dec_win.at[pl.ds(first, window), columns(c)],
                                            win_here.at[:, columns(c)], came.at[2 + c]))
    for copy in coming:
        copy.start()
    coming[0].wait()
    leaving = [pltpu.make_async_copy(lat_here, lat_out, left.at[0])]
    leaving[0].start()
    coming[1].wait()
    for c in range(steps):
        at = slice(c * wide, (c + 1) * wide)
        coming[2 + c].wait()
        value = jnp.dot(lat_here[...], win_here[:, at], preferred_element_type=jnp.float32)
        rec_here[:, at] = (value + bias_here[:, at]).astype(jnp.bfloat16)
        leaving.append(pltpu.make_async_copy(rec_here.at[:, columns(c)], rec_out.at[:, columns(c)],
                                             left.at[1 + c]))
        leaving[-1].start()
    for copy in leaving:
        copy.wait()


def on_device(acts, w_enc, b_enc, w_dec, b_dec):
    ring = lax.axis_size("tok")
    rows, width = acts.shape[1:]
    half = width // 2
    window = WINDOW * GROUP
    blocks = WINDOW + 1
    _, arrivals = sem_plan(len(column_plan(half, ENC_WIDTHS)), len(column_plan(half, DEC_WIDTHS)))
    hbm = pl.BlockSpec(memory_space=pl.ANY)
    vmem = pl.BlockSpec(memory_space=pltpu.VMEM)
    bf16, f32 = jnp.bfloat16, jnp.float32
    latents, dec_win = pl.pallas_call(
        functools.partial(kernel, ring),
        out_shape=(
            jax.ShapeDtypeStruct((rows, window), bf16),
            jax.ShapeDtypeStruct((blocks * GROUP, width), bf16),
        ),
        in_specs=[hbm, hbm, vmem, hbm],
        out_specs=(hbm, hbm),
        scratch_shapes=[
            pltpu.VMEM((2, rows, half), bf16),
            pltpu.VMEM((blocks * GROUP, half), bf16),
            pltpu.VMEM((blocks, 8, 2 * GROUP), f32),
            pltpu.VMEM((2, rows, window), f32),
            pltpu.VMEM((rows, window), f32),
            pltpu.VMEM((2, rows, window // 2), bf16),
            pltpu.VMEM((2, rows, window // 2), bf16),
            pltpu.VMEM((rows, window), bf16),
            pltpu.VMEM((6, rows // 4, window // 2), bf16),
            pltpu.VMEM((2, rows, window), bf16),
            pltpu.SemaphoreType.DMA((80,)),
            pltpu.SemaphoreType.DMA((arrivals,)),
        ],
        compiler_params=pltpu.CompilerParams(
            collective_id=0, has_side_effects=True, vmem_limit_bytes=60 * 1024 * 1024
        ),
        cost_estimate=pl.CostEstimate(
            flops=2 * rows * window * width, bytes_accessed=8 * rows * width, transcendentals=0
        ),
    )(acts[0], jnp.swapaxes(w_enc[0], 0, 1), b_enc.reshape(1, GROUP), w_dec[0])
    steps = 6 if width % 768 == 0 else 1
    latents, recon = pl.pallas_call(
        decode,
        out_shape=(
            jax.ShapeDtypeStruct((rows, window), bf16),
            jax.ShapeDtypeStruct((rows, width), bf16),
        ),
        in_specs=[hbm, hbm, hbm],
        out_specs=(hbm, hbm),
        scratch_shapes=[
            pltpu.VMEM((rows, window), bf16),
            pltpu.VMEM((window, width), bf16),
            pltpu.VMEM((1, width), f32),
            pltpu.VMEM((rows, width), bf16),
            pltpu.SemaphoreType.DMA((steps + 2,)),
            pltpu.SemaphoreType.DMA((steps + 1,)),
        ],
        compiler_params=pltpu.CompilerParams(vmem_limit_bytes=60 * 1024 * 1024),
        cost_estimate=pl.CostEstimate(
            flops=2 * rows * window * width, bytes_accessed=6 * rows * width, transcendentals=0
        ),
    )(latents, dec_win, b_dec)
    return latents, recon[None]


def solution(mesh):
    return jax.shard_map(
        on_device,
        mesh=mesh,
        in_specs=(
            P("layer", "tok", None),
            P("layer", None, "tok"),
            P("tok"),
            P("layer", "tok", None),
            P("layer", None),
        ),
        out_specs=(P("tok", None), P("layer", "tok", None)),
        check_vma=False,
    )
```

```python
import functools

import jax
import jax.numpy as jnp
from jax import lax
from jax.experimental import pallas as pl
from jax.experimental.pallas import tpu as pltpu
from jax.sharding import PartitionSpec as P

GROUP = 64
WINDOW = 8
MESH = pl.DeviceIdType.MESH
ENC_WIDTHS = [1152]
DEC_WIDTHS = [512, 384, 256]


def column_plan(half, widths):
    if half != sum(widths):
        widths = [half]
    plan, at = [], 0
    for width in widths:
        plan.append((at, width))
        at += width
    return plan


def sem_plan(enc_pieces, dec_pieces):
    sizes = dict(own=2, enc=9 * enc_pieces, acts=2, bias=5, sib=2, part=6, gather=6, lat=8,
                 kept=1, half=2, dec=4 * dec_pieces, decx=4 * dec_pieces, out=1)
    at, plan = 0, {}
    for name, size in sizes.items():
        plan[name] = at
        at += size
    return plan, at


def kernel(ring, acts, enc, bias, dec, lat_out, dec_win,
           acts_all, enc_all, bias_all, pre, total, sib_out, sib_in,
           part_out, part_in, lat, send, recv):
    rows, width = acts.shape
    half = width // 2
    quarter = rows // 4
    window = WINDOW * GROUP
    part = window // 2
    enc_plan, dec_plan = column_plan(half, ENC_WIDTHS), column_plan(half, DEC_WIDTHS)
    base, _ = sem_plan(len(enc_plan), len(dec_plan))

    layer = lax.axis_index("layer")
    tok = lax.axis_index("tok")
    g, h = layer // 2, layer % 2
    m2, s = tok - tok % 2, tok % 2
    chip = 2 * g + s
    oh, os = 1 - h, 1 - s
    alone = h == s

    def at_site(g_, h_, s_):
        return (2 * g_ + h_, m2 + s_)

    following = (layer, lax.rem(tok + 2, ring))
    before = (layer, lax.rem(tok + ring - 2, ring))
    sibling = at_site(g, oh, s)
    across = at_site(g, h, os)

    pending = []

    def remote(src, dst, target, sem):
        return pltpu.make_async_remote_copy(
            src_ref=src, dst_ref=dst, send_sem=send.at[len(pending)], recv_sem=recv.at[sem],
            device_id=target, device_id_type=MESH)

    settled = [0]

    def settle(count):
        for away, copy in pending[settled[0]:count]:
            if away is None:
                copy.wait_send()
            else:
                pl.when(away)(copy.wait_send)
        settled[0] = max(settled[0], count)

    def push(src, dst, target, sem):
        copy = remote(src, dst, target, sem)
        copy.start()
        pending.append((None, copy))

    def push_if(cond, src, dst, target, sem):
        copy = remote(src, dst, target, sem)
        pl.when(cond)(copy.start)
        pending.append((cond, copy))

    def push_or_keep(src, dst, target, sem, keep):
        away = jnp.logical_not(keep)
        copy = remote(src, dst, target, sem)

        @pl.when(away)
        def _():
            copy.start()

        @pl.when(keep)
        def _():
            pltpu.make_async_copy(src, dst, recv.at[sem]).start()

        pending.append((away, copy))

    def arrived(dst, sem):
        pltpu.make_async_copy(dst, dst, recv.at[sem]).wait()

    def lanes(d):
        return pl.ds(pl.multiple_of(d * half, half), half)

    def block(b, count=1):
        if isinstance(b, int):
            return pl.ds(b * GROUP, count * GROUP)
        return pl.ds(pl.multiple_of(b * GROUP, GROUP), count * GROUP)

    own_bias = bias[...]
    bias_all[os] = jnp.broadcast_to(jnp.concatenate([own_bias, own_bias], axis=1), (8, 2 * GROUP))

    barrier = pltpu.get_barrier_semaphore()
    me = 2 * chip + h
    for j in range(1, 8):
        other = lax.rem(me + j, 8)
        pl.semaphore_signal(barrier, inc=1, device_id=at_site(other // 4, other % 2, (other // 2) % 2),
                            device_id_type=MESH)
    pl.semaphore_signal(barrier, inc=1, device_id=before, device_id_type=MESH)
    pl.semaphore_wait(barrier, 8)

    def exchange(src, dst, sem):
        push(src.at[:, lanes(oh)], dst, at_site(g, oh, h), sem)
        push_or_keep(src.at[:, lanes(h)], dst, at_site(g, h, h), sem, alone)

    pltpu.make_async_copy(dec, dec_win.at[block(os)], recv.at[base["kept"]]).start()
    exchange(enc, enc_all.at[block(os)], base["own"] + s)
    push(bias_all.at[os], bias_all.at[os], across, base["bias"])

    def enc_part(b, e):
        off, wide = enc_plan[e]
        return enc_all.at[block(b), pl.ds(off, wide)]

    def enc_wait(b, e):
        arrived(enc_part(b, e), base["enc"] + len(enc_plan) * b + e)

    def enc_send(b, e):
        push(enc_part(b, e), enc_part(b + 2, e), following, base["enc"] + len(enc_plan) * (b + 2) + e)

    def enc_pass(b):
        for e in range(len(enc_plan)):
            enc_wait(b, e)
            enc_send(b, e)

    def enc_own(b, p, near):
        sem = base["enc"] + len(enc_plan) * (b + 2)
        if near:
            for e, (off, wide) in enumerate(enc_plan):
                here = enc.at[:, pl.ds(pl.multiple_of(h * half + off, 128), wide)]
                push_if(alone, here, enc_part(b + 2, e), following, sem + e)
        arrived(enc_all.at[block(b)], base["own"] + p)
        for e in range(len(enc_plan)):
            if near:
                push_if(jnp.logical_not(alone), enc_part(b, e), enc_part(b + 2, e), following, sem + e)
            else:
                enc_send(b, e)

    def bias_pass(i):
        if i == 0:
            arrived(bias_all.at[s], base["bias"])
        else:
            arrived(bias_all.at[pl.ds(2 * i, 2)], base["bias"] + i)
        count = 1 if i == 3 else 2
        push(bias_all.at[pl.ds(2 * i, count)], bias_all.at[pl.ds(2 * i + 2, count)], following,
             base["bias"] + i + 1)

    enc_own(os, s, True)
    enc_own(s, os, False)
    push(dec.at[:, lanes(os)], dec_win.at[block(os), lanes(os)], across, base["half"])
    exchange(acts, acts_all.at[s], base["acts"] + s)
    push_if(s == 0, dec.at[:, lanes(0)], dec_win.at[block(1), lanes(0)], across, base["half"] + 1)
    bias_pass(0)

    for i in (1, 2):
        enc_pass(2 * i + os)
        enc_pass(2 * i + s)
        bias_pass(i)
    enc_pass(6)
    bias_pass(3)

    def columns(q):
        return pl.ds(q * part, part)

    def encode(t, q):
        first = (1 - t) * GROUP + q * part
        pre[t, :, q * part:(q + 1) * part] = lax.dot_general(
            acts_all[t], enc_all[first:first + part, :], (((1,), (1,)), ((), ())),
            preferred_element_type=jnp.float32)

    def cores_send(q):
        sib_out[q] = pre[oh, :, q * part:(q + 1) * part].astype(jnp.bfloat16)
        push(sib_out.at[q], sib_in.at[q], sibling, base["sib"] + q)

    def chip_rows(c_):
        return pl.ds(pl.multiple_of(c_ * quarter, quarter), quarter)

    def chips_send(q):
        arrived(sib_in.at[q], base["sib"] + q)
        value = pre[h, :, q * part:(q + 1) * part] + sib_in[q].astype(jnp.float32)
        total[:, q * part:(q + 1) * part] = value
        part_out[:, q * part:(q + 1) * part] = value.astype(jnp.bfloat16)
        for j in (2, 1, 3):
            other = lax.rem(chip + j, 4)
            push(part_out.at[chip_rows(other), columns(q)], part_in.at[3 * q + j - 1],
                 at_site(other // 2, h, other % 2), base["part"] + 3 * q + j - 1)

    def latents_send(q):
        value = total[chip_rows(chip), q * part:(q + 1) * part] + bias_row[:, q * part:(q + 1) * part]
        for j in (1, 3, 2):
            arrived(part_in.at[3 * q + j - 1], base["part"] + 3 * q + j - 1)
            value = value + part_in[3 * q + j - 1].astype(jnp.float32)
        lat[h, chip_rows(chip), q * part:(q + 1) * part] = jnp.maximum(value, 0.0).astype(jnp.bfloat16)
        mine = lat.at[h, chip_rows(chip), columns(q)]
        for j in (2, 1, 3):
            other = lax.rem(chip + j, 4)
            push(mine, mine, at_site(other // 2, h, other % 2), base["gather"] + 3 * q + j - 1)
        push(mine, mine, sibling, base["lat"] + 4 * q)

    def latents_share(q):
        for j in (1, 3, 2):
            piece = lat.at[h, chip_rows(lax.rem(chip + 4 - j, 4)), columns(q)]
            arrived(piece, base["gather"] + 3 * q + j - 1)
            push(piece, piece, sibling, base["lat"] + 4 * q + j)

    def latents_wait(q):
        for j in (0, 1, 3, 2):
            arrived(lat.at[oh, chip_rows(lax.rem(chip + 4 - j, 4)), columns(q)], base["lat"] + 4 * q + j)

    def dec_part(b, count, c, side):
        off, wide = dec_plan[c]
        return dec_win.at[pl.ds(b * GROUP, count * GROUP),
                          pl.ds(pl.multiple_of(side * half + off, 128), wide)]

    def dec_sem(kind, i, c):
        return base[kind] + len(dec_plan) * (i - 1) + c

    def dec_pass(i, pieces=range(len(dec_plan))):
        count = 1 if i == 3 else 2
        for c in pieces:
            if i > 0:
                arrived(dec_part(2 * i, 2, c, s), dec_sem("dec", i, c))
            push(dec_part(2 * i, count, c, s), dec_part(2 * i + 2, count, c, s), following,
                 dec_sem("dec", i + 1, c))
            if i > 0:
                push(dec_part(2 * i, 2, c, s), dec_part(2 * i, 2, c, s), across, dec_sem("decx", i, c))

    arrived(dec_win.at[block(os)], base["kept"])
    arrived(dec_win.at[block(s), lanes(s)], base["half"])
    dec_pass(0)

    arrived(acts_all.at[0], base["acts"])
    arrived(acts_all.at[1], base["acts"] + 1)
    encode(1, 0)
    encode(0, 0)
    cores_send(0)
    for e in range(len(enc_plan)):
        enc_wait(7, e)
    encode(1, 1)
    arrived(bias_all.at[pl.ds(8, 1)], base["bias"] + 4)
    low = lax.broadcasted_iota(jnp.int32, (1, 2 * GROUP), 1) < GROUP
    bias_row = jnp.concatenate(
        [jnp.where(low, bias_all[oh + k, 0:1, :], bias_all[oh + k + 1, 0:1, :])
         for k in range(0, WINDOW, 2)], axis=1)
    chips_send(0)
    for e in range(len(enc_plan)):
        enc_wait(8, e)
    encode(0, 1)
    cores_send(1)
    sent = len(pending)
    dec_pass(1, [0])
    chips_send(1)
    dec_pass(1, [1])
    latents_send(0)
    dec_pass(1, range(2, len(dec_plan)))
    latents_send(1)
    latents_share(0)
    dec_pass(2, [0])
    dec_pass(2, [1])
    latents_share(1)
    dec_pass(2, range(2, len(dec_plan)))
    settle(sent)
    sent = len(pending)
    dec_pass(3)
    latents_wait(0)
    latents_wait(1)
    latents_copy = pltpu.make_async_copy(lat.at[s], lat_out, recv.at[base["out"]])
    latents_copy.start()
    for c in range(len(dec_plan)):
        arrived(dec_part(8, 1, c, s), dec_sem("dec", 4, c))
        push_if(s == 1, dec_part(8, 1, c, 1), dec_part(8, 1, c, 1), across, dec_sem("decx", 4, c))
    settle(sent)

    @pl.when(s == 1)
    def _():
        arrived(dec_win.at[block(1), lanes(0)], base["half"] + 1)

    for i in (1, 2, 3):
        for c in range(len(dec_plan)):
            arrived(dec_part(2 * i, 2, c, os), dec_sem("decx", i, c))

    @pl.when(s == 0)
    def _():
        for c in range(len(dec_plan)):
            arrived(dec_part(8, 1, c, 1), dec_sem("decx", 4, c))

    latents_copy.wait()
    settle(len(pending))


def decode(lat, dec_win, bdec, lat_out, rec_out, lat_here, win_here, bias_here, rec_here, came, left):
    window = lat.shape[1]
    first = pl.multiple_of((1 - lax.axis_index("tok") % 2) * GROUP, GROUP)
    steps = came.shape[0] - 2
    wide = dec_win.shape[1] // steps

    def columns(c):
        return pl.ds(c * wide, wide)

    coming = [pltpu.make_async_copy(lat, lat_here, came.at[0]), pltpu.make_async_copy(bdec, bias_here, came.at[1])]
    for c in range(steps):
        coming.append(pltpu.make_async_copy(dec_win.at[pl.ds(first, window), columns(c)],
                                            win_here.at[:, columns(c)], came.at[2 + c]))
    for copy in coming:
        copy.start()
    coming[0].wait()
    leaving = [pltpu.make_async_copy(lat_here, lat_out, left.at[0])]
    leaving[0].start()
    coming[1].wait()
    for c in range(steps):
        at = slice(c * wide, (c + 1) * wide)
        coming[2 + c].wait()
        value = jnp.dot(lat_here[...], win_here[:, at], preferred_element_type=jnp.float32)
        rec_here[:, at] = (value + bias_here[:, at]).astype(jnp.bfloat16)
        leaving.append(pltpu.make_async_copy(rec_here.at[:, columns(c)], rec_out.at[:, columns(c)],
                                             left.at[1 + c]))
        leaving[-1].start()
    for copy in leaving:
        copy.wait()


def on_device(acts, w_enc, b_enc, w_dec, b_dec):
    ring = lax.axis_size("tok")
    rows, width = acts.shape[1:]
    half = width // 2
    window = WINDOW * GROUP
    blocks = WINDOW + 1
    _, arrivals = sem_plan(len(column_plan(half, ENC_WIDTHS)), len(column_plan(half, DEC_WIDTHS)))
    hbm = pl.BlockSpec(memory_space=pl.ANY)
    vmem = pl.BlockSpec(memory_space=pltpu.VMEM)
    bf16, f32 = jnp.bfloat16, jnp.float32
    latents, dec_win = pl.pallas_call(
        functools.partial(kernel, ring),
        out_shape=(
            jax.ShapeDtypeStruct((rows, window), bf16),
            jax.ShapeDtypeStruct((blocks * GROUP, width), bf16),
        ),
        in_specs=[hbm, hbm, vmem, hbm],
        out_specs=(hbm, hbm),
        scratch_shapes=[
            pltpu.VMEM((2, rows, half), bf16),
            pltpu.VMEM((blocks * GROUP, half), bf16),
            pltpu.VMEM((blocks, 8, 2 * GROUP), f32),
            pltpu.VMEM((2, rows, window), f32),
            pltpu.VMEM((rows, window), f32),
            pltpu.VMEM((2, rows, window // 2), bf16),
            pltpu.VMEM((2, rows, window // 2), bf16),
            pltpu.VMEM((rows, window), bf16),
            pltpu.VMEM((6, rows // 4, window // 2), bf16),
            pltpu.VMEM((2, rows, window), bf16),
            pltpu.SemaphoreType.DMA((80,)),
            pltpu.SemaphoreType.DMA((arrivals,)),
        ],
        compiler_params=pltpu.CompilerParams(
            collective_id=0, has_side_effects=True, vmem_limit_bytes=60 * 1024 * 1024
        ),
        cost_estimate=pl.CostEstimate(
            flops=2 * rows * window * width, bytes_accessed=8 * rows * width, transcendentals=0
        ),
    )(acts[0], jnp.swapaxes(w_enc[0], 0, 1), b_enc.reshape(1, GROUP), w_dec[0])
    steps = 6 if width % 768 == 0 else 1
    latents, recon = pl.pallas_call(
        decode,
        out_shape=(
            jax.ShapeDtypeStruct((rows, window), bf16),
            jax.ShapeDtypeStruct((rows, width), bf16),
        ),
        in_specs=[hbm, hbm, hbm],
        out_specs=(hbm, hbm),
        scratch_shapes=[
            pltpu.VMEM((rows, window), bf16),
            pltpu.VMEM((window, width), bf16),
            pltpu.VMEM((1, width), f32),
            pltpu.VMEM((rows, width), bf16),
            pltpu.SemaphoreType.DMA((steps + 2,)),
            pltpu.SemaphoreType.DMA((steps + 1,)),
        ],
        compiler_params=pltpu.CompilerParams(vmem_limit_bytes=60 * 1024 * 1024),
        cost_estimate=pl.CostEstimate(
            flops=2 * rows * window * width, bytes_accessed=6 * rows * width, transcendentals=0
        ),
    )(latents, dec_win, b_dec)
    return latents, recon[None]


def solution(mesh):
    return jax.shard_map(
        on_device,
        mesh=mesh,
        in_specs=(
            P("layer", "tok", None),
            P("layer", None, "tok"),
            P("tok"),
            P("layer", "tok", None),
            P("layer", None),
        ),
        out_specs=(P("tok", None), P("layer", "tok", None)),
        check_vma=False,
    )
```
